256 devices in a mesh: tok: 16 (over y, z_lo), tp: 16 (over z_hi, x, core).
Axes of the slice: x: 4, y: 4, z: 8 (z_hi: 2, z_lo: 4; z = z_hi * 4 + z_lo), core: 2. Of those that a mesh axis runs over, the one named last changes fastest.
Arguments:
- hidden: bfloat16 [16384, 28672], P('tok', 'tp'), may hold values from -48 to 48, as said below
- signs: int32 [28672], P('tp'), may hold values from 0 to 1
Outputs:
- gram: float32 [28672, 128], P(('tok', 'tp'))
The draws below stay inside these ranges and needn't reach their ends.
Inputs may be any that keep to these rules, and one draw needn't show every extreme that they name: `hidden`: Activations; finite.
All inputs are finite; a program needn't handle non-finite values.
Results may differ from the reference program's by a relative error of at most 0.0046.
Values may be sent and summed in bfloat16 or wider, within the bound.
No kernel may reach another device: no remote copies, remote signals or barrier semaphores. Data moves between devices by JAX's collectives and lax.ppermute only.
A program may use at most 64 MiB of HBM per device.

```python
import math
import jax
import jax.numpy as jnp
import numpy as np
from jax import lax

FF = 28672
HAD_BIG = 1024
HAD_SMALL = 28
COLS = 128
TOK_DEV = 64
TOKENS = 16384
N_TOK = 16
N_TP = 16


def draw_hidden(key, part):
    key = jax.random.fold_in(key, 7)
    noise_key, column_key, row_key = jax.random.split(key, 3)
    noise = jnp.clip(jax.random.normal(noise_key, (TOKENS, FF), jnp.float32), -4.0, 4.0)
    columns = jnp.exp(jax.random.uniform(column_key, (1, FF), jnp.float32, jnp.log(0.3), jnp.log(3.0)))
    row_scale = jnp.exp(jax.random.uniform(row_key, (TOKENS, 1), jnp.float32, jnp.log(0.4), jnp.log(4.0)))
    values = noise * columns * row_scale
    return values.astype(jnp.bfloat16)


def place_ends(result, stream_key, least, top_value):
    dims = result.shape
    spot = [jax.random.randint(jax.random.fold_in(stream_key, axis), (), 0, dims[axis]) for axis in range(len(dims))]
    result = result.at[tuple(spot)].set(least)
    longest = dims.index(max(dims))
    spot[longest] = (spot[longest] + 1) % dims[longest]
    return result.at[tuple(spot)].set(top_value)


def setup_inputs(seed: int = 0) -> dict:
    streams_of = jax.random.split(jax.random.key(seed), 3)
    hidden = draw_hidden(jax.random.fold_in(streams_of[2], 71), 0)
    signs = place_ends(jax.random.randint(streams_of[1], (FF,), 0, 2), jax.random.fold_in(streams_of[1], 1), 0, 1).astype(jnp.int32)
    return {"hidden": hidden, "signs": signs}


def paley_table():
    modulus = 13
    residue_set = set((number * number % modulus for number in range(1, modulus)))
    character = np.array([0.0] + [1.0 if number in residue_set else -1.0 for number in range(1, modulus)], dtype=np.float32)
    offsets = (np.arange(modulus)[None, :] - np.arange(modulus)[:, None]) % modulus
    jacobsthal = character[offsets]
    top_row = np.concatenate([np.zeros((1, 1), np.float32), np.ones((1, modulus), np.float32)], axis=1)
    lower_rows = np.concatenate([np.ones((modulus, 1), np.float32), jacobsthal], axis=1)
    conference = np.concatenate([top_row, lower_rows], axis=0)
    pair_one = np.array([[1.0, 1.0], [1.0, -1.0]], np.float32)
    pair_two = np.array([[1.0, -1.0], [-1.0, -1.0]], np.float32)
    table = np.kron(conference, pair_one) + np.kron(np.eye(modulus + 1, dtype=np.float32), pair_two)
    return table.astype(np.float32)

def sylvester_table(order):
    table = np.ones((1, 1), np.float32)
    basic = np.array([[1.0, 1.0], [1.0, -1.0]], np.float32)
    while table.shape[0] < order:
        table = np.kron(table, basic).astype(np.float32)
    return jnp.asarray(table, jnp.float32)

def reference(hidden, signs):
    sign_row = (1 - 2 * signs).astype(jnp.bfloat16)
    small_table = jnp.asarray(paley_table(), jnp.float32)
    big_table = sylvester_table(HAD_BIG)
    factor = 1.0 / math.sqrt(FF)
    block_rows = TOK_DEV * N_TP

    def accumulate(total, position):
        piece = lax.dynamic_slice_in_dim(hidden, (position * block_rows).astype(jnp.int32), block_rows, 0)
        signed = (piece * sign_row[None, :]).astype(jnp.bfloat16)
        cube = signed.reshape(block_rows, HAD_SMALL, HAD_BIG).astype(jnp.float32)
        first = jnp.einsum('rab,cb->rac', cube, big_table).astype(jnp.bfloat16)
        second = jnp.einsum('rab,ca->rcb', first.astype(jnp.float32), small_table) * factor
        rotated = second.astype(jnp.bfloat16).reshape(block_rows, FF)
        term = jnp.dot(rotated.T, rotated[:, :COLS], preferred_element_type=jnp.float32)
        return (total + term, None)
    start_total = jnp.zeros((FF, COLS), jnp.float32)
    total, unused = lax.scan(accumulate, start_total, jnp.arange(N_TOK, dtype=jnp.int32))
    return total / TOKENS
```

```python
import functools

import jax
import jax.numpy as jnp
import numpy as np
from jax import lax
from jax.experimental import pallas as pl
from jax.experimental.pallas import tpu as pltpu
from jax.sharding import Mesh, PartitionSpec as P

FF = 28672
TOKENS = 16384
BIG = 1024
SMALL = 28
COLS = 128
BLK = 256
N_TP = 16
N_TOK = 16
N_XC = 8
WIDTH = FF // N_TP
N_Q = WIDTH // BLK
ROWS = FF // (N_TP * N_TOK)
TOK = TOKENS // N_TOK
HALF = TOK // 2
GROUP = COLS // N_TOK
LANE = 128

BF = jnp.bfloat16
F32 = jnp.float32


def paley_table():
    modulus = 13
    residues = {n * n % modulus for n in range(1, modulus)}
    character = np.array(
        [0.0] + [1.0 if n in residues else -1.0 for n in range(1, modulus)], np.float32
    )
    offsets = (np.arange(modulus)[None, :] - np.arange(modulus)[:, None]) % modulus
    lower = np.concatenate([np.ones((modulus, 1), np.float32), character[offsets]], axis=1)
    top = np.concatenate([np.zeros((1, 1), np.float32), np.ones((1, modulus), np.float32)], axis=1)
    conference = np.concatenate([top, lower], axis=0)
    one = np.array([[1.0, 1.0], [1.0, -1.0]], np.float32)
    two = np.array([[1.0, -1.0], [-1.0, -1.0]], np.float32)
    return np.kron(conference, one) + np.kron(np.eye(modulus + 1, dtype=np.float32), two)


def sylvester(order):
    table = np.ones((1, 1), np.float32)
    while table.shape[0] < order:
        table = np.kron(table, np.array([[1.0, 1.0], [1.0, -1.0]], np.float32))
    return table


def fold_table():
    return np.repeat(paley_table()[0], BIG).reshape(N_TP, 1, WIDTH)


def window_table():
    h = sylvester(BLK)
    out = np.zeros((N_XC, BLK, 2, LANE), np.float32)
    for pl_ in range(N_XC):
        for z in range(2):
            start = ROWS * (pl_ + N_XC * z)
            out[pl_, :, z, :] = h[:, (start + np.arange(LANE)) % BLK]
    return out.reshape(N_XC, BLK, 2 * LANE)


def mix_table():
    q_all = np.kron(paley_table(), sylvester(4))
    n_q = q_all.shape[0]
    out = np.zeros((N_TP, 2, 2, N_TOK, N_Q, N_XC), np.float32)
    for p in range(N_TP):
        zh, pl_ = divmod(p, N_XC)
        for z in range(2):
            first = ROWS * (pl_ + N_XC * z) // BLK
            for v in range(2):
                i = min(first + v, N_Q - 1)
                for j in range(N_Q):
                    for m in range(N_XC):
                        q = (zh * N_XC + m) * N_Q + j
                        out[p, z, v, :, j, m] = q_all[np.arange(N_TOK) * N_Q + i, q]
    assert n_q == N_TOK * N_Q
    return out


def mix_big_table():
    small = mix_table()
    eye = np.eye(GROUP, dtype=np.float32)
    big = np.einsum("pzvkjm,ab->pzvkajmb", small, eye)
    return big.reshape(N_TP, 2 * 2 * N_TOK * GROUP, N_Q * N_XC * GROUP)


def fold_kernel(ids, x_ref, s_ref, w_ref, send_ref, keep_ref):
    step = pl.program_id(0)
    coef = (1 - 2 * s_ref[...]).astype(F32) * w_ref[0]
    rows = x_ref.shape[0]
    total = jnp.zeros((rows, LANE), F32)
    for j in range(WIDTH // LANE):
        cols = slice(j * LANE, (j + 1) * LANE)
        total = total + x_ref[:, cols].astype(F32) * coef[:, cols]

    per = HALF // rows

    @pl.when(step < per)
    def _():
        send_ref[pl.ds(pl.multiple_of(step * rows, rows), rows), :] = total.astype(BF)

    @pl.when(step >= per)
    def _():
        keep_ref[pl.ds(pl.multiple_of((step - per) * rows, rows), rows), :] = total


def fold(ids, hidden, signs, weights):
    rows = 256
    per = HALF // rows

    def place(i, ids):
        core = ids[1]
        half = jnp.where(i < per, 1 - core, core)
        return (half * per + i % per, 0)

    return pl.pallas_call(
        fold_kernel,
        grid_spec=pltpu.PrefetchScalarGridSpec(
            num_scalar_prefetch=1,
            grid=(TOK // rows,),
            in_specs=[
                pl.BlockSpec((rows, WIDTH), place),
                pl.BlockSpec((1, WIDTH), lambda i, ids: (0, 0)),
                pl.BlockSpec((1, 1, WIDTH), lambda i, ids: (ids[0], 0, 0)),
            ],
            out_specs=[
                pl.BlockSpec((HALF, LANE), lambda i, ids: (0, 0)),
                pl.BlockSpec((HALF, LANE), lambda i, ids: (0, 0)),
            ],
        ),
        out_shape=[
            jax.ShapeDtypeStruct((HALF, LANE), BF),
            jax.ShapeDtypeStruct((HALF, LANE), F32),
        ],
        name="fold",
    )(ids, hidden, signs, weights)


def outer_kernel(ids, mine, mine_z, other, other_z, x_ref, out_ref):
    core = ids[1]
    dims = (((0,), (0,)), ((), ()))
    dot = functools.partial(lax.dot_general, dimension_numbers=dims, preferred_element_type=F32)
    x_mine = x_ref[pl.ds(pl.multiple_of(core * HALF, HALF), HALF), :]
    x_other = x_ref[pl.ds(pl.multiple_of((1 - core) * HALF, HALF), HALF), :]
    total = dot(mine[...], x_mine) + dot(mine_z[...], x_mine)
    total = total + dot(other[...], x_other) + dot(other_z[...], x_other)
    out_ref[...] = total.astype(BF)


def outer(ids, mine, mine_z, other, other_z, hidden):
    tile = 256
    whole = pl.BlockSpec((HALF, LANE), lambda i, ids: (0, 0))
    return pl.pallas_call(
        outer_kernel,
        grid_spec=pltpu.PrefetchScalarGridSpec(
            num_scalar_prefetch=1,
            grid=(WIDTH // tile,),
            in_specs=[whole] * 4 + [pl.BlockSpec((TOK, tile), lambda i, ids: (0, i))],
            out_specs=pl.BlockSpec((COLS, tile), lambda i, ids: (0, i)),
        ),
        out_shape=jax.ShapeDtypeStruct((COLS, WIDTH), BF),
        name="outer",
    )(ids, mine, mine_z, other, other_z, hidden)


def gather_kernel(x_ref, s_ref, out_ref):
    terms = x_ref[...].astype(F32).reshape(N_TOK, GROUP, WIDTH)
    total = jnp.sum(terms, axis=0) * (1 - 2 * s_ref[...]).astype(F32)
    out_ref[...] = jnp.concatenate([total] * N_XC, axis=0).astype(BF)


def gathered(x, signs):
    return pl.pallas_call(
        gather_kernel,
        out_shape=jax.ShapeDtypeStruct((N_XC * GROUP, WIDTH), BF),
        name="sum_tok",
    )(x, signs)


def split_dot(lhs, value):
    high = value.astype(BF)
    low = (value - high.astype(F32)).astype(BF)
    dot = functools.partial(jnp.dot, preferred_element_type=F32)
    return dot(lhs, high) + dot(lhs, low)


def rotate_kernel(ids, g_ref, win_ref, mix_ref, out_ref):
    window = win_ref[0]
    parts = []
    for j in range(N_Q):
        block = g_ref[:, j * BLK : (j + 1) * BLK]
        parts.append(jnp.dot(block, window, preferred_element_type=F32))
    spread = jnp.concatenate(parts, axis=0)
    lanes = lax.broadcasted_iota(jnp.int32, (N_TOK * GROUP, LANE), 1)
    halves = []
    for z in range(2):
        start = ROWS * (ids[0] % N_XC + N_XC * z)
        both = split_dot(
            mix_ref[0, z * 2 * LANE : (z + 1) * 2 * LANE, :], spread[:, z * LANE : (z + 1) * LANE]
        )
        wrapped = start % BLK + lanes >= BLK
        mixed = jnp.where(wrapped, both[LANE:], both[:LANE])
        halves.append(mixed.reshape(N_TOK, 1, GROUP, LANE))
    out_ref[...] = jnp.concatenate(halves, axis=1).reshape(2 * N_TOK * GROUP, LANE)


def rotate(ids, g, windows, mix):
    return pl.pallas_call(
        rotate_kernel,
        grid_spec=pltpu.PrefetchScalarGridSpec(
            num_scalar_prefetch=1,
            grid=(1,),
            in_specs=[
                pl.BlockSpec((N_XC * GROUP, WIDTH), lambda i, ids: (0, 0)),
                pl.BlockSpec((1, BLK, 2 * LANE), lambda i, ids: (ids[0] % N_XC, 0, 0)),
                pl.BlockSpec(
                    (1, 4 * N_TOK * GROUP, N_Q * N_XC * GROUP), lambda i, ids: (ids[0], 0, 0)
                ),
            ],
            out_specs=pl.BlockSpec((2 * N_TOK * GROUP, LANE), lambda i, ids: (0, 0)),
        ),
        out_shape=jax.ShapeDtypeStruct((2 * N_TOK * GROUP, LANE), F32),
        name="rotate",
    )(ids, g, windows, mix)


def finish_kernel(x_ref, h_ref, out_ref):
    terms = x_ref[...].reshape(N_TOK, 2, GROUP, LANE)
    total = (terms[:, 0] + terms[:, 1]).reshape(COLS, LANE) * (1.0 / (FF * TOKENS))
    dims = (((0,), (0,)), ((), ()))
    dot = functools.partial(lax.dot_general, dimension_numbers=dims, preferred_element_type=F32)
    high = total.astype(BF)
    rest = total - high.astype(F32)
    mid = rest.astype(BF)
    low = (rest - mid.astype(F32)).astype(BF)
    table = h_ref[...]
    result = dot(high, table) + (dot(mid, table) + dot(low, table))
    out_ref[...] = result[:ROWS]


def finish(x, table):
    return pl.pallas_call(
        finish_kernel,
        out_shape=jax.ShapeDtypeStruct((ROWS, COLS), F32),
        name="finish",
    )(x, table)


TOK_AXES = ("y", "zl")
TP_AXES = ("zh", "x", "core")


def body(hidden, signs):
    p = lax.axis_index(TP_AXES).astype(jnp.int32)
    core = lax.axis_index("core").astype(jnp.int32)
    ids = jnp.stack([p, core])
    signs = signs.reshape(1, WIDTH)
    send, keep = fold(ids, hidden, signs, jnp.asarray(fold_table(), F32))

    swap = [(0, 1), (1, 0)]
    near = [(i, i ^ 1) for i in range(4)]
    far = [(i, i ^ 2) for i in range(4)]
    total = keep + lax.ppermute(send, "core", swap).astype(F32)
    total = total + lax.ppermute(total.astype(BF), "x", near).astype(F32)
    total = total + lax.ppermute(total.astype(BF), "x", far).astype(F32)
    mine = total.astype(BF)
    mine_z = lax.ppermute(mine, "zh", swap)
    other = lax.ppermute(mine, "core", swap)
    other_z = lax.ppermute(mine_z, "core", swap)

    wide = outer(ids, mine, mine_z, other, other_z, hidden)
    wide = lax.all_to_all(wide, TOK_AXES, split_axis=0, concat_axis=0, tiled=True)
    g = gathered(wide, signs)
    g = lax.all_to_all(g, ("x", "core"), split_axis=0, concat_axis=0, tiled=True)
    turned = rotate(ids, g, jnp.asarray(window_table(), BF), jnp.asarray(mix_big_table(), BF))
    turned = lax.all_to_all(turned, ("y", "zl", "zh"), split_axis=0, concat_axis=0, tiled=True)
    return finish(turned, jnp.asarray(sylvester(COLS), BF))


def solution(mesh):
    fine = Mesh(mesh.devices.reshape(4, 4, 2, 4, 2), ("y", "zl", "zh", "x", "core"))
    return jax.shard_map(
        body,
        mesh=fine,
        in_specs=(P(TOK_AXES, TP_AXES), P(TP_AXES)),
        out_specs=P(TOK_AXES + TP_AXES, None),
        check_vma=False,
    )
```

```python
import functools

import jax
import jax.numpy as jnp
import numpy as np
from jax import lax
from jax.experimental import pallas as pl
from jax.experimental.pallas import tpu as pltpu
from jax.sharding import Mesh, PartitionSpec as P

FF = 28672
TOKENS = 16384
BIG = 1024
SMALL = 28
COLS = 128
BLK = 256
N_TP = 16
N_TOK = 16
N_XC = 8
RING = 4
WIDTH = FF // N_TP
N_Q = WIDTH // BLK
ROWS = FF // (N_TP * N_TOK)
TOK = TOKENS // N_TOK
HALF = TOK // 2
GROUP = COLS // N_TOK
LANE = 128
N_L = WIDTH // LANE
FOLDED = WIDTH // 2

BF = jnp.bfloat16
F32 = jnp.float32
TOK_AXES = ("y", "zl")
TP_AXES = ("zh", "x", "core")
VMEM = pl.BlockSpec(memory_space=pltpu.VMEM)
HBM = pl.BlockSpec(memory_space=pltpu.HBM)
LITTLE = pltpu.CompilerParams(vmem_limit_bytes=8 << 20)


def paley_table():
    modulus = 13
    residues = {n * n % modulus for n in range(1, modulus)}
    character = np.array(
        [0.0] + [1.0 if n in residues else -1.0 for n in range(1, modulus)], np.float32
    )
    offsets = (np.arange(modulus)[None, :] - np.arange(modulus)[:, None]) % modulus
    lower = np.concatenate([np.ones((modulus, 1), np.float32), character[offsets]], axis=1)
    top = np.concatenate([np.zeros((1, 1), np.float32), np.ones((1, modulus), np.float32)], axis=1)
    conference = np.concatenate([top, lower], axis=0)
    one = np.array([[1.0, 1.0], [1.0, -1.0]], np.float32)
    two = np.array([[1.0, -1.0], [-1.0, -1.0]], np.float32)
    return np.kron(conference, one) + np.kron(np.eye(modulus + 1, dtype=np.float32), two)


def sylvester(order):
    table = np.ones((1, 1), np.float32)
    while table.shape[0] < order:
        table = np.kron(table, np.array([[1.0, 1.0], [1.0, -1.0]], np.float32))
    return table


def window_table():
    h = sylvester(BLK)
    out = np.zeros((N_XC, BLK, 2, LANE), np.float32)
    for member in range(N_XC):
        for z in range(2):
            start = ROWS * (member + N_XC * z)
            out[member, :, z, :] = h[:, (start + np.arange(LANE)) % BLK]
    return out.reshape(N_XC, BLK, 2 * LANE)


def mix_table():
    q_all = np.kron(paley_table(), sylvester(BIG // BLK))
    small = np.zeros((N_TP, 2, 2, N_TOK, N_Q, N_XC), np.float32)
    for p in range(N_TP):
        zh, member = divmod(p, N_XC)
        x, core = divmod(member, 2)
        for z in range(2):
            first = ROWS * (member + N_XC * z) // BLK
            for v in range(2):
                i = min(first + v, N_Q - 1)
                for j in range(N_Q):
                    for slot in range(N_XC):
                        s, e = divmod(slot, 2)
                        source = ((x - s) % RING) * 2 + (core ^ e)
                        q = (zh * N_XC + source) * N_Q + j
                        small[p, z, v, :, j, slot] = q_all[np.arange(N_TOK) * N_Q + i, q]
    eye = np.eye(GROUP, dtype=np.float32)
    big = np.einsum("pzvkjm,ab->pzvkajmb", small, eye)
    return big.reshape(N_TP, 4 * LANE, N_Q * N_XC * GROUP)


def in_hbm(x):
    return pltpu.with_memory_space_constraint(x, pltpu.HBM)


def fold_kernel(x_ref, s_ref, send_ref, keep_ref, held_ref, sign_ref, raw, sems, sign_sem):
    core = lax.axis_index("core")
    p = lax.axis_index("zh") * N_XC + lax.axis_index("x") * 2 + core
    sign_copy = pltpu.make_async_copy(s_ref, raw, sign_sem)
    sign_copy.start()
    rows = FOLD_ROWS
    count = TOK // rows
    per = count // 2
    copies, starts = [], []
    for i in range(count):
        half = 1 - core if i < per else core
        start = pl.multiple_of(half * HALF + (i % per) * rows, rows)
        here = pl.ds(start, rows)
        copy = pltpu.make_async_copy(x_ref.at[here, :], held_ref.at[here, :], sems.at[i])
        copy.start()
        copies.append(copy)
        starts.append(here)
    sign_copy.wait()
    first_row = paley_table()[0]
    coefs = []
    for j in range(N_L):
        block = (p * N_L + j) // (BIG // LANE)
        weight = jnp.float32(1.0)
        for a in range(SMALL):
            if first_row[a] != 1.0:
                weight = jnp.where(block == a, jnp.float32(first_row[a]), weight)
        sign = (1 - 2 * raw[j : j + 1, :]).astype(F32)
        sign_ref[j : j + 1, :] = sign
        coefs.append(sign * weight)
    for i in range(count):
        copies[i].wait()
        total = jnp.zeros((rows, LANE), F32)
        for j in range(N_L):
            total = total + held_ref[starts[i], j * LANE : (j + 1) * LANE].astype(F32) * coefs[j]
        place = slice((i % per) * rows, (i % per + 1) * rows)
        if i < per:
            send_ref[place, :] = total.astype(BF)
        else:
            keep_ref[place, :] = total


FOLD_ROWS = 128


def fold(hidden, signs):
    count = TOK // FOLD_ROWS
    return pl.pallas_call(
        fold_kernel,
        in_specs=[HBM, HBM],
        out_specs=[VMEM] * 4,
        out_shape=[
            jax.ShapeDtypeStruct((HALF, LANE), BF),
            jax.ShapeDtypeStruct((HALF, LANE), F32),
            jax.ShapeDtypeStruct((TOK, WIDTH), BF),
            jax.ShapeDtypeStruct((N_L, LANE), F32),
        ],
        scratch_shapes=[
            pltpu.VMEM((N_L, LANE), jnp.int32),
            pltpu.SemaphoreType.DMA((count,)),
            pltpu.SemaphoreType.DMA,
        ],
        compiler_params=LITTLE,
        cost_estimate=pl.CostEstimate(
            flops=2 * TOK * WIDTH, bytes_accessed=2 * TOK * WIDTH, transcendentals=0
        ),
        name="fold",
    )(in_hbm(hidden), in_hbm(signs))


def sum_core_kernel(own, a, out_ref, short_ref):
    total = own[...] + a[...].astype(F32)
    out_ref[...] = total
    short_ref[...] = total.astype(BF)


def sum_core(own, term):
    return pl.pallas_call(
        sum_core_kernel,
        in_specs=[VMEM] * 2,
        out_specs=[VMEM] * 2,
        out_shape=[
            jax.ShapeDtypeStruct((HALF, LANE), F32),
            jax.ShapeDtypeStruct((HALF, LANE), BF),
        ],
        compiler_params=LITTLE,
        name="sum_core",
    )(own, term)


def sum_x_kernel(own, a, b, c, out_ref):
    total = (own[...] + a[...].astype(F32)) + (b[...].astype(F32) + c[...].astype(F32))
    out_ref[...] = total.T.astype(BF)


def sum_x(own, terms):
    return pl.pallas_call(
        sum_x_kernel,
        in_specs=[VMEM] * 4,
        out_specs=VMEM,
        out_shape=jax.ShapeDtypeStruct((LANE, HALF), BF),
        compiler_params=LITTLE,
        name="sum_x",
    )(own, *terms)


def tiles(ref):
    for i in range(N_Q):
        yield slice(i * BLK, (i + 1) * BLK), ref[:, i * BLK : (i + 1) * BLK]


def outer_kernel(mine, other, x_ref, out_ref):
    core = lax.axis_index("core")
    mine, other = mine[...], other[...]
    left = jnp.concatenate(
        [jnp.where(core == 0, mine, other), jnp.where(core == 0, other, mine)], axis=1
    )
    for cols, block in tiles(x_ref):
        out_ref[:, cols] = jnp.dot(left, block, preferred_element_type=F32)


def cost(tokens):
    return pl.CostEstimate(
        flops=2 * COLS * tokens * WIDTH, bytes_accessed=2 * tokens * WIDTH, transcendentals=0
    )


def outer(mine, other, hidden):
    return pl.pallas_call(
        outer_kernel,
        in_specs=[VMEM] * 3,
        out_specs=VMEM,
        out_shape=jax.ShapeDtypeStruct((COLS, WIDTH), F32),
        compiler_params=LITTLE,
        cost_estimate=cost(TOK),
        name="outer",
    )(mine, other, hidden)


def half_of(x_ref, half):
    return x_ref.at[pl.ds(pl.multiple_of(half * HALF, HALF), HALF), :]


def outer_mine_kernel(mine, acc_ref, x_ref, out_ref):
    left = mine[...]
    for cols, block in tiles(half_of(x_ref, lax.axis_index("core"))):
        out_ref[:, cols] = acc_ref[:, cols] + jnp.dot(left, block, preferred_element_type=F32)


def outer_mine(mine, acc, hidden):
    return pl.pallas_call(
        outer_mine_kernel,
        in_specs=[VMEM] * 3,
        out_specs=VMEM,
        out_shape=jax.ShapeDtypeStruct((COLS, WIDTH), F32),
        compiler_params=LITTLE,
        cost_estimate=cost(HALF),
        name="outer_mine",
    )(mine, acc, hidden)


def outer_other_kernel(other, acc_ref, x_ref, own_ref, s1_ref, s2_ref, s3_ref, total):
    left = other[...]
    y = lax.axis_index("y")
    per = COLS // RING
    for cols, block in tiles(half_of(x_ref, 1 - lax.axis_index("core"))):
        total[:, cols] = acc_ref[:, cols] + jnp.dot(left, block, preferred_element_type=F32)
    for s, ref in enumerate((own_ref, s1_ref, s2_ref, s3_ref)):
        start = pl.multiple_of((y + s) % RING * per, per)
        ref[...] = total[pl.ds(start, per), :].astype(ref.dtype)


def outer_other(other, acc, hidden):
    per = COLS // RING
    return pl.pallas_call(
        outer_other_kernel,
        in_specs=[VMEM] * 3,
        out_specs=[VMEM] * RING,
        out_shape=[jax.ShapeDtypeStruct((per, WIDTH), F32)]
        + [jax.ShapeDtypeStruct((per, WIDTH), BF)] * (RING - 1),
        scratch_shapes=[pltpu.VMEM((COLS, WIDTH), F32)],
        compiler_params=LITTLE,
        cost_estimate=cost(HALF),
        name="outer_other",
    )(other, acc, hidden)


def pack(x):
    return jnp.concatenate([x[:, :FOLDED], x[:, FOLDED:]], axis=0)


def unpack(x):
    x = x.astype(F32)
    return jnp.concatenate([x[:GROUP], x[GROUP:]], axis=1)


def sum_y_kernel(own, a, b, c, own_ref, s1_ref, s2_ref, s3_ref, total):
    total[...] = (own[...] + a[...].astype(F32)) + (b[...].astype(F32) + c[...].astype(F32))
    zl = lax.axis_index("zl")
    for s, ref in enumerate((own_ref, s1_ref, s2_ref, s3_ref)):
        start = pl.multiple_of((zl + s) % RING * GROUP, GROUP)
        part = total[pl.ds(start, GROUP), :]
        if s == 0:
            ref[...] = part
        else:
            ref[...] = pack(part).astype(BF)


def sum_y(own, terms):
    return pl.pallas_call(
        sum_y_kernel,
        in_specs=[VMEM] * RING,
        out_specs=[VMEM] * RING,
        out_shape=[jax.ShapeDtypeStruct((GROUP, WIDTH), F32)]
        + [jax.ShapeDtypeStruct((2 * GROUP, FOLDED), BF)] * (RING - 1),
        scratch_shapes=[pltpu.VMEM((COLS // RING, WIDTH), F32)],
        compiler_params=LITTLE,
        name="sum_y",
    )(own, *terms)


def sum_z_kernel(own, a, b, c, s_ref, out_ref):
    total = (own[...] + unpack(a[...])) + (unpack(b[...]) + unpack(c[...]))
    sign = jnp.concatenate([s_ref[j : j + 1, :] for j in range(N_L)], axis=1)
    out_ref[...] = pack(total * sign).astype(BF)


def sum_z(own, terms, signs):
    return pl.pallas_call(
        sum_z_kernel,
        in_specs=[VMEM] * (RING + 1),
        out_specs=VMEM,
        out_shape=jax.ShapeDtypeStruct((2 * GROUP, FOLDED), BF),
        compiler_params=LITTLE,
        name="sum_z",
    )(own, *terms, signs)


def split_dot(lhs, value):
    high = value.astype(BF)
    low = (value - high.astype(F32)).astype(BF)
    dot = functools.partial(jnp.dot, preferred_element_type=F32)
    return dot(lhs, high) + dot(lhs, low)


def tables_kernel(win_hbm, mix_hbm, win_ref, mix_ref, sems):
    member = lax.axis_index("x") * 2 + lax.axis_index("core")
    p = lax.axis_index("zh") * N_XC + member
    copies = [
        pltpu.make_async_copy(win_hbm.at[member], win_ref, sems.at[0]),
        pltpu.make_async_copy(mix_hbm.at[p], mix_ref, sems.at[1]),
    ]
    for copy in copies:
        copy.start()
    for copy in copies:
        copy.wait()


def tables():
    return pl.pallas_call(
        tables_kernel,
        in_specs=[HBM, HBM],
        out_specs=[VMEM, VMEM],
        out_shape=[
            jax.ShapeDtypeStruct((BLK, 2 * LANE), BF),
            jax.ShapeDtypeStruct((4 * LANE, N_Q * N_XC * GROUP), BF),
        ],
        scratch_shapes=[pltpu.SemaphoreType.DMA((2,))],
        compiler_params=LITTLE,
        name="tables",
    )(in_hbm(jnp.asarray(window_table(), BF)), in_hbm(jnp.asarray(mix_table(), BF)))


def rotate_kernel(*refs):
    slots, (win_ref, mix_ref, out_ref) = refs[:N_XC], refs[N_XC:]
    member = lax.axis_index("x") * 2 + lax.axis_index("core")
    g = jnp.concatenate([unpack(ref[...]) for ref in slots], axis=0).astype(BF)
    window = win_ref[...]
    parts = []
    for j in range(N_Q):
        parts.append(
            jnp.dot(g[:, j * BLK : (j + 1) * BLK], window, preferred_element_type=F32)
        )
    spread = jnp.concatenate(parts, axis=0)
    lanes = lax.broadcasted_iota(jnp.int32, (LANE, LANE), 1)
    halves = []
    for z in range(2):
        start = ROWS * (member + N_XC * z)
        both = split_dot(
            mix_ref[z * 2 * LANE : (z + 1) * 2 * LANE, :], spread[:, z * LANE : (z + 1) * LANE]
        )
        wrapped = start % BLK + lanes >= BLK
        mixed = jnp.where(wrapped, both[LANE:], both[:LANE])
        halves.append(mixed.reshape(N_TOK, 1, GROUP, LANE))
    out_ref[...] = jnp.concatenate(halves, axis=1).reshape(2 * LANE, LANE)


def rotate(slots, window, mix):
    return pl.pallas_call(
        rotate_kernel,
        in_specs=[VMEM] * (N_XC + 2),
        out_specs=VMEM,
        out_shape=jax.ShapeDtypeStruct((2 * LANE, LANE), F32),
        compiler_params=LITTLE,
        name="rotate",
    )(*slots, window, mix)


def finish_kernel(x_ref, h_ref, out_ref):
    terms = x_ref[...].reshape(N_TOK, 2, GROUP, LANE)
    total = (terms[:, 0] + terms[:, 1]).reshape(COLS, LANE) * (1.0 / (FF * TOKENS))
    dims = (((0,), (0,)), ((), ()))
    dot = functools.partial(lax.dot_general, dimension_numbers=dims, preferred_element_type=F32)
    high = total.astype(BF)
    rest = total - high.astype(F32)
    mid = rest.astype(BF)
    low = (rest - mid.astype(F32)).astype(BF)
    table = h_ref[...]
    result = dot(high, table) + (dot(mid, table) + dot(low, table))
    out_ref[...] = result[:ROWS]


def finish(x, table):
    return pl.pallas_call(
        finish_kernel,
        in_specs=[VMEM, VMEM],
        out_specs=VMEM,
        out_shape=jax.ShapeDtypeStruct((ROWS, COLS), F32),
        compiler_params=LITTLE,
        name="finish",
    )(x, table)


def shift(x, axis, s):
    return lax.ppermute(x, axis, [(i, (i + s) % RING) for i in range(RING)])


def swap(x, axis):
    return lax.ppermute(x, axis, [(0, 1), (1, 0)])


def body(hidden, signs):
    send, keep, held, sign = fold(hidden, signs.reshape(N_L, LANE))
    pair, short = sum_core(keep, swap(send, "core"))
    mine = sum_x(pair, [shift(short, "x", s) for s in (1, 2, 3)])
    mine_z = swap(mine, "zh")
    acc = outer(mine, swap(mine, "core"), held)
    acc = outer_mine(mine_z, acc, held)
    own, *sends = outer_other(swap(mine_z, "core"), acc, held)

    own, *sends = sum_y(own, [shift(x, "y", s + 1) for s, x in enumerate(sends)])
    g = sum_z(own, [shift(x, "zl", s + 1) for s, x in enumerate(sends)], sign)

    ring = [g] + [shift(g, "x", s) for s in (1, 2, 3)]
    slots = [part for x in ring for part in (x, swap(x, "core"))]
    turned = rotate(slots, *tables())
    turned = lax.all_to_all(turned, ("y", "zl", "zh"), split_axis=0, concat_axis=0, tiled=True)
    return finish(turned, jnp.asarray(sylvester(COLS), BF))


def solution(mesh):
    fine = Mesh(mesh.devices.reshape(4, 4, 2, 4, 2), ("y", "zl", "zh", "x", "core"))
    return jax.shard_map(
        body,
        mesh=fine,
        in_specs=(P(TOK_AXES, TP_AXES), P(TP_AXES)),
        out_specs=P(TOK_AXES + TP_AXES, None),
        check_vma=False,
    )
```

```python
import functools

import jax
import jax.numpy as jnp
import numpy as np
from jax import lax
from jax.experimental import pallas as pl
from jax.experimental.pallas import tpu as pltpu
from jax.sharding import Mesh, PartitionSpec as P

FF = 28672
TOKENS = 16384
BIG = 1024
SMALL = 28
COLS = 128
BLK = 256
N_TP = 16
N_TOK = 16
N_XC = 8
RING = 4
WIDTH = FF // N_TP
N_Q = WIDTH // BLK
ROWS = FF // (N_TP * N_TOK)
TOK = TOKENS // N_TOK
HALF = TOK // 2
GROUP = COLS // N_TOK
LANE = 128
N_L = WIDTH // LANE
FOLDED = WIDTH // 2

BF = jnp.bfloat16
F32 = jnp.float32
TOK_AXES = ("y", "zl")
TP_AXES = ("zh", "x", "core")
VMEM = pl.BlockSpec(memory_space=pltpu.VMEM)
HBM = pl.BlockSpec(memory_space=pltpu.HBM)
LITTLE = pltpu.CompilerParams(vmem_limit_bytes=8 << 20)


def paley_table():
    modulus = 13
    residues = {n * n % modulus for n in range(1, modulus)}
    character = np.array(
        [0.0] + [1.0 if n in residues else -1.0 for n in range(1, modulus)], np.float32
    )
    offsets = (np.arange(modulus)[None, :] - np.arange(modulus)[:, None]) % modulus
    lower = np.concatenate([np.ones((modulus, 1), np.float32), character[offsets]], axis=1)
    top = np.concatenate([np.zeros((1, 1), np.float32), np.ones((1, modulus), np.float32)], axis=1)
    conference = np.concatenate([top, lower], axis=0)
    one = np.array([[1.0, 1.0], [1.0, -1.0]], np.float32)
    two = np.array([[1.0, -1.0], [-1.0, -1.0]], np.float32)
    return np.kron(conference, one) + np.kron(np.eye(modulus + 1, dtype=np.float32), two)


def sylvester(order):
    table = np.ones((1, 1), np.float32)
    while table.shape[0] < order:
        table = np.kron(table, np.array([[1.0, 1.0], [1.0, -1.0]], np.float32))
    return table


def window_table():
    h = sylvester(BLK)
    out = np.zeros((N_XC, BLK, 2, LANE), np.float32)
    for member in range(N_XC):
        for z in range(2):
            start = ROWS * (member + N_XC * z)
            out[member, :, z, :] = h[:, (start + np.arange(LANE)) % BLK]
    return out.reshape(N_XC, BLK, 2 * LANE)


def mix_table():
    q_all = np.kron(paley_table(), sylvester(BIG // BLK))
    small = np.zeros((N_TP, 2, 2, N_TOK, N_Q, N_XC), np.float32)
    for p in range(N_TP):
        zh, member = divmod(p, N_XC)
        x, core = divmod(member, 2)
        for z in range(2):
            first = ROWS * (member + N_XC * z) // BLK
            for v in range(2):
                i = min(first + v, N_Q - 1)
                for j in range(N_Q):
                    for slot in range(N_XC):
                        s, e = divmod(slot, 2)
                        source = ((x - s) % RING) * 2 + (core ^ e)
                        q = (zh * N_XC + source) * N_Q + j
                        small[p, z, v, :, j, slot] = q_all[np.arange(N_TOK) * N_Q + i, q]
    eye = np.eye(GROUP, dtype=np.float32)
    big = np.einsum("pzvkjm,ab->pzvkajmb", small, eye)
    return big.reshape(N_TP, 4 * LANE, N_Q * N_XC * GROUP)


def in_hbm(x):
    return pltpu.with_memory_space_constraint(x, pltpu.HBM)


def fold_kernel(x_ref, s_ref, send_ref, keep_ref, held_ref, sign_ref, raw, sems, sign_sem):
    core = lax.axis_index("core")
    p = lax.axis_index("zh") * N_XC + lax.axis_index("x") * 2 + core
    sign_copy = pltpu.make_async_copy(s_ref, raw, sign_sem)
    sign_copy.start()
    rows = FOLD_ROWS
    count = TOK // rows
    per = count // 2
    copies, starts = [], []
    for i in range(count):
        half = 1 - core if i < per else core
        start = pl.multiple_of(half * HALF + (i % per) * rows, rows)
        here = pl.ds(start, rows)
        copy = pltpu.make_async_copy(x_ref.at[here, :], held_ref.at[here, :], sems.at[i])
        copy.start()
        copies.append(copy)
        starts.append(here)
    sign_copy.wait()
    first_row = paley_table()[0]
    coefs = []
    for j in range(N_L):
        block = (p * N_L + j) // (BIG // LANE)
        weight = jnp.float32(1.0)
        for a in range(SMALL):
            if first_row[a] != 1.0:
                weight = jnp.where(block == a, jnp.float32(first_row[a]), weight)
        sign = (1 - 2 * raw[j : j + 1, :]).astype(F32)
        sign_ref[j : j + 1, :] = sign
        coefs.append(sign * weight)
    for i in range(count):
        copies[i].wait()
        total = jnp.zeros((rows, LANE), F32)
        for j in range(N_L):
            total = total + held_ref[starts[i], j * LANE : (j + 1) * LANE].astype(F32) * coefs[j]
        place = slice((i % per) * rows, (i % per + 1) * rows)
        if i < per:
            send_ref[place, :] = total.astype(BF)
        else:
            keep_ref[place, :] = total


FOLD_ROWS = 128


def fold(hidden, signs):
    count = TOK // FOLD_ROWS
    return pl.pallas_call(
        fold_kernel,
        in_specs=[HBM, HBM],
        out_specs=[VMEM] * 4,
        out_shape=[
            jax.ShapeDtypeStruct((HALF, LANE), BF),
            jax.ShapeDtypeStruct((HALF, LANE), F32),
            jax.ShapeDtypeStruct((TOK, WIDTH), BF),
            jax.ShapeDtypeStruct((N_L, LANE), F32),
        ],
        scratch_shapes=[
            pltpu.VMEM((N_L, LANE), jnp.int32),
            pltpu.SemaphoreType.DMA((count,)),
            pltpu.SemaphoreType.DMA,
        ],
        compiler_params=LITTLE,
        cost_estimate=pl.CostEstimate(
            flops=2 * TOK * WIDTH, bytes_accessed=2 * TOK * WIDTH, transcendentals=0
        ),
        name="fold",
    )(in_hbm(hidden), in_hbm(signs))


def sum_core_kernel(own, a, out_ref, short_ref):
    total = own[...] + a[...].astype(F32)
    out_ref[...] = total
    short_ref[...] = total.astype(BF)


def sum_core(own, term):
    return pl.pallas_call(
        sum_core_kernel,
        in_specs=[VMEM] * 2,
        out_specs=[VMEM] * 2,
        out_shape=[
            jax.ShapeDtypeStruct((HALF, LANE), F32),
            jax.ShapeDtypeStruct((HALF, LANE), BF),
        ],
        compiler_params=LITTLE,
        name="sum_core",
    )(own, term)


def sum_x_kernel(own, a, b, c, out_ref):
    total = (own[...] + a[...].astype(F32)) + (b[...].astype(F32) + c[...].astype(F32))
    out_ref[...] = total.T.astype(BF)


def sum_x(own, terms):
    return pl.pallas_call(
        sum_x_kernel,
        in_specs=[VMEM] * 4,
        out_specs=VMEM,
        out_shape=jax.ShapeDtypeStruct((LANE, HALF), BF),
        compiler_params=LITTLE,
        name="sum_x",
    )(own, *terms)


def tiles(ref):
    for i in range(N_Q):
        yield slice(i * BLK, (i + 1) * BLK), ref[:, i * BLK : (i + 1) * BLK]


def outer_kernel(mine, other, x_ref, out_ref):
    core = lax.axis_index("core")
    mine, other = mine[...], other[...]
    left = jnp.concatenate(
        [jnp.where(core == 0, mine, other), jnp.where(core == 0, other, mine)], axis=1
    )
    for cols, block in tiles(x_ref):
        out_ref[:, cols] = jnp.dot(left, block, preferred_element_type=F32)


def cost(tokens):
    return pl.CostEstimate(
        flops=2 * COLS * tokens * WIDTH, bytes_accessed=2 * tokens * WIDTH, transcendentals=0
    )


def outer(mine, other, hidden):
    return pl.pallas_call(
        outer_kernel,
        in_specs=[VMEM] * 3,
        out_specs=VMEM,
        out_shape=jax.ShapeDtypeStruct((COLS, WIDTH), F32),
        compiler_params=LITTLE,
        cost_estimate=cost(TOK),
        name="outer",
    )(mine, other, hidden)


def half_of(x_ref, half):
    return x_ref.at[pl.ds(pl.multiple_of(half * HALF, HALF), HALF), :]


def outer_mine_kernel(mine, acc_ref, x_ref, out_ref):
    left = mine[...]
    for cols, block in tiles(half_of(x_ref, lax.axis_index("core"))):
        out_ref[:, cols] = acc_ref[:, cols] + jnp.dot(left, block, preferred_element_type=F32)


def outer_mine(mine, acc, hidden):
    return pl.pallas_call(
        outer_mine_kernel,
        in_specs=[VMEM] * 3,
        out_specs=VMEM,
        out_shape=jax.ShapeDtypeStruct((COLS, WIDTH), F32),
        compiler_params=LITTLE,
        cost_estimate=cost(HALF),
        name="outer_mine",
    )(mine, acc, hidden)


def outer_other_kernel(other, acc_ref, x_ref, own_ref, s1_ref, s2_ref, s3_ref, total):
    left = other[...]
    y = lax.axis_index("y")
    per = COLS // RING
    for cols, block in tiles(half_of(x_ref, 1 - lax.axis_index("core"))):
        total[:, cols] = acc_ref[:, cols] + jnp.dot(left, block, preferred_element_type=F32)
    for s, ref in enumerate((own_ref, s1_ref, s2_ref, s3_ref)):
        start = pl.multiple_of((y + s) % RING * per, per)
        ref[...] = total[pl.ds(start, per), :].astype(ref.dtype)


def outer_other(other, acc, hidden):
    per = COLS // RING
    return pl.pallas_call(
        outer_other_kernel,
        in_specs=[VMEM] * 3,
        out_specs=[VMEM] * RING,
        out_shape=[jax.ShapeDtypeStruct((per, WIDTH), F32)]
        + [jax.ShapeDtypeStruct((per, WIDTH), BF)] * (RING - 1),
        scratch_shapes=[pltpu.VMEM((COLS, WIDTH), F32)],
        compiler_params=LITTLE,
        cost_estimate=cost(HALF),
        name="outer_other",
    )(other, acc, hidden)


def pack(x):
    return jnp.concatenate([x[:, :FOLDED], x[:, FOLDED:]], axis=0)


def unpack(x):
    x = x.astype(F32)
    return jnp.concatenate([x[:GROUP], x[GROUP:]], axis=1)


def sum_y_kernel(own, a, b, c, own_ref, s1_ref, s2_ref, s3_ref, total):
    total[...] = (own[...] + a[...].astype(F32)) + (b[...].astype(F32) + c[...].astype(F32))
    zl = lax.axis_index("zl")
    for s, ref in enumerate((own_ref, s1_ref, s2_ref, s3_ref)):
        start = pl.multiple_of((zl + s) % RING * GROUP, GROUP)
        part = total[pl.ds(start, GROUP), :]
        if s == 0:
            ref[...] = part
        else:
            ref[...] = pack(part).astype(BF)


def sum_y(own, terms):
    return pl.pallas_call(
        sum_y_kernel,
        in_specs=[VMEM] * RING,
        out_specs=[VMEM] * RING,
        out_shape=[jax.ShapeDtypeStruct((GROUP, WIDTH), F32)]
        + [jax.ShapeDtypeStruct((2 * GROUP, FOLDED), BF)] * (RING - 1),
        scratch_shapes=[pltpu.VMEM((COLS // RING, WIDTH), F32)],
        compiler_params=LITTLE,
        name="sum_y",
    )(own, *terms)


def sum_z_kernel(own, a, b, c, s_ref, out_ref):
    total = (own[...] + unpack(a[...])) + (unpack(b[...]) + unpack(c[...]))
    sign = jnp.concatenate([s_ref[j : j + 1, :] for j in range(N_L)], axis=1)
    out_ref[...] = pack(total * sign).astype(BF)


def sum_z(own, terms, signs):
    return pl.pallas_call(
        sum_z_kernel,
        in_specs=[VMEM] * (RING + 1),
        out_specs=VMEM,
        out_shape=jax.ShapeDtypeStruct((2 * GROUP, FOLDED), BF),
        compiler_params=LITTLE,
        name="sum_z",
    )(own, *terms, signs)


def split_dot(lhs, value):
    high = value.astype(BF)
    low = (value - high.astype(F32)).astype(BF)
    dot = functools.partial(jnp.dot, preferred_element_type=F32)
    return dot(lhs, high) + dot(lhs, low)


def tables_kernel(win_hbm, mix_hbm, win_ref, mix_ref, sems):
    member = lax.axis_index("x") * 2 + lax.axis_index("core")
    p = lax.axis_index("zh") * N_XC + member
    copies = [
        pltpu.make_async_copy(win_hbm.at[member], win_ref, sems.at[0]),
        pltpu.make_async_copy(mix_hbm.at[p], mix_ref, sems.at[1]),
    ]
    for copy in copies:
        copy.start()
    for copy in copies:
        copy.wait()


def tables():
    return pl.pallas_call(
        tables_kernel,
        in_specs=[HBM, HBM],
        out_specs=[VMEM, VMEM],
        out_shape=[
            jax.ShapeDtypeStruct((BLK, 2 * LANE), BF),
            jax.ShapeDtypeStruct((4 * LANE, N_Q * N_XC * GROUP), BF),
        ],
        scratch_shapes=[pltpu.SemaphoreType.DMA((2,))],
        compiler_params=LITTLE,
        name="tables",
    )(in_hbm(jnp.asarray(window_table(), BF)), in_hbm(jnp.asarray(mix_table(), BF)))


def rotate_kernel(*refs):
    slots, (win_ref, mix_ref, out_ref) = refs[:N_XC], refs[N_XC:]
    member = lax.axis_index("x") * 2 + lax.axis_index("core")
    g = jnp.concatenate([unpack(ref[...]) for ref in slots], axis=0).astype(BF)
    window = win_ref[...]
    parts = []
    for j in range(N_Q):
        parts.append(
            jnp.dot(g[:, j * BLK : (j + 1) * BLK], window, preferred_element_type=F32)
        )
    spread = jnp.concatenate(parts, axis=0)
    lanes = lax.broadcasted_iota(jnp.int32, (LANE, LANE), 1)
    halves = []
    for z in range(2):
        start = ROWS * (member + N_XC * z)
        both = split_dot(
            mix_ref[z * 2 * LANE : (z + 1) * 2 * LANE, :], spread[:, z * LANE : (z + 1) * LANE]
        )
        wrapped = start % BLK + lanes >= BLK
        mixed = jnp.where(wrapped, both[LANE:], both[:LANE])
        halves.append(mixed.reshape(N_TOK, 1, GROUP, LANE))
    out_ref[...] = jnp.concatenate(halves, axis=1).reshape(2 * LANE, LANE)


def rotate(slots, window, mix):
    return pl.pallas_call(
        rotate_kernel,
        in_specs=[VMEM] * (N_XC + 2),
        out_specs=VMEM,
        out_shape=jax.ShapeDtypeStruct((2 * LANE, LANE), F32),
        compiler_params=LITTLE,
        name="rotate",
    )(*slots, window, mix)


def finish_kernel(x_ref, h_ref, out_ref):
    terms = x_ref[...].reshape(N_TOK, 2, GROUP, LANE)
    total = (terms[:, 0] + terms[:, 1]).reshape(COLS, LANE) * (1.0 / (FF * TOKENS))
    dims = (((0,), (0,)), ((), ()))
    dot = functools.partial(lax.dot_general, dimension_numbers=dims, preferred_element_type=F32)
    high = total.astype(BF)
    rest = total - high.astype(F32)
    mid = rest.astype(BF)
    low = (rest - mid.astype(F32)).astype(BF)
    table = h_ref[...]
    result = dot(high, table) + (dot(mid, table) + dot(low, table))
    out_ref[...] = result[:ROWS]


def finish(x, table):
    return pl.pallas_call(
        finish_kernel,
        in_specs=[VMEM, VMEM],
        out_specs=VMEM,
        out_shape=jax.ShapeDtypeStruct((ROWS, COLS), F32),
        compiler_params=LITTLE,
        name="finish",
    )(x, table)


def shift(x, axis, s):
    return lax.ppermute(x, axis, [(i, (i + s) % RING) for i in range(RING)])


def swap(x, axis):
    return lax.ppermute(x, axis, [(0, 1), (1, 0)])


def body(hidden, signs):
    send, keep, held, sign = fold(hidden, signs.reshape(N_L, LANE))
    pair, short = sum_core(keep, swap(send, "core"))
    mine = sum_x(pair, [shift(short, "x", s) for s in (1, 3, 2)])
    mine_z = swap(mine, "zh")
    acc = outer(mine, swap(mine, "core"), held)
    acc = outer_mine(mine_z, acc, held)
    own, *sends = outer_other(swap(mine_z, "core"), acc, held)

    own, *sends = sum_y(own, [shift(sends[s - 1], "y", s) for s in (1, 3, 2)])
    g = sum_z(own, [shift(x, "zl", s + 1) for s, x in enumerate(sends)], sign)

    ring = [g] + [shift(g, "x", s) for s in (1, 2, 3)]
    slots = [part for x in ring for part in (x, swap(x, "core"))]
    turned = rotate(slots, *tables())
    turned = lax.all_to_all(turned, ("y", "zl", "zh"), split_axis=0, concat_axis=0, tiled=True)
    return finish(turned, jnp.asarray(sylvester(COLS), BF))


def solution(mesh):
    fine = Mesh(mesh.devices.reshape(4, 4, 2, 4, 2), ("y", "zl", "zh", "x", "core"))
    return jax.shard_map(
        body,
        mesh=fine,
        in_specs=(P(TOK_AXES, TP_AXES), P(TP_AXES)),
        out_specs=P(TOK_AXES + TP_AXES, None),
        check_vma=False,
    )
```

```python
import functools

import jax
import jax.numpy as jnp
import numpy as np
from jax import lax
from jax.experimental import pallas as pl
from jax.experimental.pallas import tpu as pltpu
from jax.sharding import Mesh, PartitionSpec as P

FF = 28672
TOKENS = 16384
BIG = 1024
SMALL = 28
COLS = 128
BLK = 256
N_TP = 16
N_TOK = 16
N_XC = 8
RING = 4
WIDTH = FF // N_TP
N_Q = WIDTH // BLK
ROWS = FF // (N_TP * N_TOK)
TOK = TOKENS // N_TOK
HALF = TOK // 2
GROUP = COLS // N_TOK
LANE = 128
N_L = WIDTH // LANE
FOLDED = WIDTH // 2

BF = jnp.bfloat16
F32 = jnp.float32
TOK_AXES = ("y", "zl")
TP_AXES = ("zh", "x", "core")
VMEM = pl.BlockSpec(memory_space=pltpu.VMEM)
HBM = pl.BlockSpec(memory_space=pltpu.HBM)
LITTLE = pltpu.CompilerParams(vmem_limit_bytes=8 << 20)


def paley_table():
    modulus = 13
    residues = {n * n % modulus for n in range(1, modulus)}
    character = np.array(
        [0.0] + [1.0 if n in residues else -1.0 for n in range(1, modulus)], np.float32
    )
    offsets = (np.arange(modulus)[None, :] - np.arange(modulus)[:, None]) % modulus
    lower = np.concatenate([np.ones((modulus, 1), np.float32), character[offsets]], axis=1)
    top = np.concatenate([np.zeros((1, 1), np.float32), np.ones((1, modulus), np.float32)], axis=1)
    conference = np.concatenate([top, lower], axis=0)
    one = np.array([[1.0, 1.0], [1.0, -1.0]], np.float32)
    two = np.array([[1.0, -1.0], [-1.0, -1.0]], np.float32)
    return np.kron(conference, one) + np.kron(np.eye(modulus + 1, dtype=np.float32), two)


def sylvester(order):
    table = np.ones((1, 1), np.float32)
    while table.shape[0] < order:
        table = np.kron(table, np.array([[1.0, 1.0], [1.0, -1.0]], np.float32))
    return table


def window_table():
    h = sylvester(BLK)
    out = np.zeros((N_XC, BLK, 2, LANE), np.float32)
    for member in range(N_XC):
        for z in range(2):
            start = ROWS * (member + N_XC * z)
            out[member, :, z, :] = h[:, (start + np.arange(LANE)) % BLK]
    return out.reshape(N_XC, BLK, 2 * LANE)


def mix_table():
    q_all = np.kron(paley_table(), sylvester(BIG // BLK))
    small = np.zeros((N_TP, 2, 2, N_TOK, N_Q, N_XC), np.float32)
    for p in range(N_TP):
        zh, member = divmod(p, N_XC)
        x, core = divmod(member, 2)
        for z in range(2):
            first = ROWS * (member + N_XC * z) // BLK
            for v in range(2):
                i = min(first + v, N_Q - 1)
                for j in range(N_Q):
                    for slot in range(N_XC):
                        s, e = divmod(slot, 2)
                        source = ((x - s) % RING) * 2 + (core ^ e)
                        q = (zh * N_XC + source) * N_Q + j
                        small[p, z, v, :, j, slot] = q_all[np.arange(N_TOK) * N_Q + i, q]
    eye = np.eye(GROUP, dtype=np.float32)
    big = np.einsum("pzvkjm,ab->pzvkajmb", small, eye)
    return big.reshape(N_TP, 4 * LANE, N_Q * N_XC * GROUP)


def in_hbm(x):
    return pltpu.with_memory_space_constraint(x, pltpu.HBM)


def fold_kernel(x_ref, s_ref, send_ref, keep_ref, held_ref, sign_ref, raw, sems, sign_sem):
    core = lax.axis_index("core")
    p = lax.axis_index("zh") * N_XC + lax.axis_index("x") * 2 + core
    sign_copy = pltpu.make_async_copy(s_ref, raw, sign_sem)
    sign_copy.start()
    rows = FOLD_ROWS
    count = TOK // rows
    per = count // 2
    copies, starts = [], []
    for i in range(count):
        half = 1 - core if i < per else core
        start = pl.multiple_of(half * HALF + (i % per) * rows, rows)
        here = pl.ds(start, rows)
        copy = pltpu.make_async_copy(x_ref.at[here, :], held_ref.at[here, :], sems.at[i])
        copy.start()
        copies.append(copy)
        starts.append(here)
    sign_copy.wait()
    first_row = paley_table()[0]
    coefs = []
    for j in range(N_L):
        block = (p * N_L + j) // (BIG // LANE)
        weight = jnp.float32(1.0)
        for a in range(SMALL):
            if first_row[a] != 1.0:
                weight = jnp.where(block == a, jnp.float32(first_row[a]), weight)
        sign = (1 - 2 * raw[j : j + 1, :]).astype(F32)
        sign_ref[j : j + 1, :] = sign
        coefs.append(sign * weight)
    for i in range(count):
        copies[i].wait()
        total = jnp.zeros((rows, LANE), F32)
        for j in range(N_L):
            total = total + held_ref[starts[i], j * LANE : (j + 1) * LANE].astype(F32) * coefs[j]
        place = slice((i % per) * rows, (i % per + 1) * rows)
        if i < per:
            send_ref[place, :] = total.astype(BF)
        else:
            keep_ref[place, :] = total


FOLD_ROWS = 128


def fold(hidden, signs):
    count = TOK // FOLD_ROWS
    return pl.pallas_call(
        fold_kernel,
        in_specs=[HBM, HBM],
        out_specs=[VMEM] * 4,
        out_shape=[
            jax.ShapeDtypeStruct((HALF, LANE), BF),
            jax.ShapeDtypeStruct((HALF, LANE), F32),
            jax.ShapeDtypeStruct((TOK, WIDTH), BF),
            jax.ShapeDtypeStruct((N_L, LANE), F32),
        ],
        scratch_shapes=[
            pltpu.VMEM((N_L, LANE), jnp.int32),
            pltpu.SemaphoreType.DMA((count,)),
            pltpu.SemaphoreType.DMA,
        ],
        compiler_params=LITTLE,
        cost_estimate=pl.CostEstimate(
            flops=2 * TOK * WIDTH, bytes_accessed=2 * TOK * WIDTH, transcendentals=0
        ),
        name="fold",
    )(in_hbm(hidden), in_hbm(signs))


def sum_core_kernel(own, a, out_ref, short_ref):
    total = own[...] + a[...].astype(F32)
    out_ref[...] = total
    short_ref[...] = total.astype(BF)


def sum_core(own, term):
    return pl.pallas_call(
        sum_core_kernel,
        in_specs=[VMEM] * 2,
        out_specs=[VMEM] * 2,
        out_shape=[
            jax.ShapeDtypeStruct((HALF, LANE), F32),
            jax.ShapeDtypeStruct((HALF, LANE), BF),
        ],
        compiler_params=LITTLE,
        name="sum_core",
    )(own, term)


def sum_x_kernel(own, a, b, c, out_ref):
    total = (own[...] + a[...].astype(F32)) + (b[...].astype(F32) + c[...].astype(F32))
    out_ref[...] = total.T.astype(BF)


def sum_x(own, terms):
    return pl.pallas_call(
        sum_x_kernel,
        in_specs=[VMEM] * 4,
        out_specs=VMEM,
        out_shape=jax.ShapeDtypeStruct((LANE, HALF), BF),
        compiler_params=LITTLE,
        name="sum_x",
    )(own, *terms)


def tiles(ref):
    for i in range(N_Q):
        yield slice(i * BLK, (i + 1) * BLK), ref[:, i * BLK : (i + 1) * BLK]


def outer_kernel(mine, other, x_ref, out_ref):
    core = lax.axis_index("core")
    mine, other = mine[...], other[...]
    left = jnp.concatenate(
        [jnp.where(core == 0, mine, other), jnp.where(core == 0, other, mine)], axis=1
    )
    for cols, block in tiles(x_ref):
        out_ref[:, cols] = jnp.dot(left, block, preferred_element_type=F32)


def cost(tokens):
    return pl.CostEstimate(
        flops=2 * COLS * tokens * WIDTH, bytes_accessed=2 * tokens * WIDTH, transcendentals=0
    )


def outer(mine, other, hidden):
    return pl.pallas_call(
        outer_kernel,
        in_specs=[VMEM] * 3,
        out_specs=VMEM,
        out_shape=jax.ShapeDtypeStruct((COLS, WIDTH), F32),
        compiler_params=LITTLE,
        cost_estimate=cost(TOK),
        name="outer",
    )(mine, other, hidden)


def half_of(x_ref, half):
    return x_ref.at[pl.ds(pl.multiple_of(half * HALF, HALF), HALF), :]


def outer_mine_kernel(mine, acc_ref, x_ref, out_ref):
    left = mine[...]
    for cols, block in tiles(half_of(x_ref, lax.axis_index("core"))):
        out_ref[:, cols] = acc_ref[:, cols] + jnp.dot(left, block, preferred_element_type=F32)


def outer_mine(mine, acc, hidden):
    return pl.pallas_call(
        outer_mine_kernel,
        in_specs=[VMEM] * 3,
        out_specs=VMEM,
        out_shape=jax.ShapeDtypeStruct((COLS, WIDTH), F32),
        compiler_params=LITTLE,
        cost_estimate=cost(HALF),
        name="outer_mine",
    )(mine, acc, hidden)


def outer_other_kernel(other, acc_ref, x_ref, own_ref, s1_ref, s2_ref, s3_ref, total):
    left = other[...]
    y = lax.axis_index("y")
    per = COLS // RING
    for cols, block in tiles(half_of(x_ref, 1 - lax.axis_index("core"))):
        total[:, cols] = acc_ref[:, cols] + jnp.dot(left, block, preferred_element_type=F32)
    for s, ref in enumerate((own_ref, s1_ref, s2_ref, s3_ref)):
        start = pl.multiple_of((y + s) % RING * per, per)
        ref[...] = total[pl.ds(start, per), :].astype(ref.dtype)


def outer_other(other, acc, hidden):
    per = COLS // RING
    return pl.pallas_call(
        outer_other_kernel,
        in_specs=[VMEM] * 3,
        out_specs=[VMEM] * RING,
        out_shape=[jax.ShapeDtypeStruct((per, WIDTH), F32)]
        + [jax.ShapeDtypeStruct((per, WIDTH), BF)] * (RING - 1),
        scratch_shapes=[pltpu.VMEM((COLS, WIDTH), F32)],
        compiler_params=LITTLE,
        cost_estimate=cost(HALF),
        name="outer_other",
    )(other, acc, hidden)


def pack(x):
    return jnp.concatenate([x[:, :FOLDED], x[:, FOLDED:]], axis=0)


def unpack(x):
    x = x.astype(F32)
    return jnp.concatenate([x[:GROUP], x[GROUP:]], axis=1)


def sum_y_kernel(own, a, b, c, own_ref, s1_ref, s2_ref, s3_ref, total):
    total[...] = (own[...] + a[...].astype(F32)) + (b[...].astype(F32) + c[...].astype(F32))
    zl = lax.axis_index("zl")
    for s, ref in enumerate((own_ref, s1_ref, s2_ref, s3_ref)):
        start = pl.multiple_of((zl + s) % RING * GROUP, GROUP)
        part = total[pl.ds(start, GROUP), :]
        if s == 0:
            ref[...] = part
        else:
            ref[...] = pack(part).astype(BF)


def sum_y(own, terms):
    return pl.pallas_call(
        sum_y_kernel,
        in_specs=[VMEM] * RING,
        out_specs=[VMEM] * RING,
        out_shape=[jax.ShapeDtypeStruct((GROUP, WIDTH), F32)]
        + [jax.ShapeDtypeStruct((2 * GROUP, FOLDED), BF)] * (RING - 1),
        scratch_shapes=[pltpu.VMEM((COLS // RING, WIDTH), F32)],
        compiler_params=LITTLE,
        name="sum_y",
    )(own, *terms)


def sum_z_kernel(own, a, b, c, s_ref, out_ref):
    total = (own[...] + unpack(a[...])) + (unpack(b[...]) + unpack(c[...]))
    sign = jnp.concatenate([s_ref[j : j + 1, :] for j in range(N_L)], axis=1)
    out_ref[...] = pack(total * sign).astype(BF)


def sum_z(own, terms, signs):
    return pl.pallas_call(
        sum_z_kernel,
        in_specs=[VMEM] * (RING + 1),
        out_specs=VMEM,
        out_shape=jax.ShapeDtypeStruct((2 * GROUP, FOLDED), BF),
        compiler_params=LITTLE,
        name="sum_z",
    )(own, *terms, signs)


def pair_kernel(a, b, out_ref):
    out_ref[...] = jnp.concatenate([a[...], b[...]], axis=0)


def pair_up(a, b):
    return pl.pallas_call(
        pair_kernel,
        in_specs=[VMEM] * 2,
        out_specs=VMEM,
        out_shape=jax.ShapeDtypeStruct((4 * GROUP, FOLDED), BF),
        compiler_params=LITTLE,
        name="pair",
    )(a, b)


def split_dot(lhs, value):
    high = value.astype(BF)
    low = (value - high.astype(F32)).astype(BF)
    dot = functools.partial(jnp.dot, preferred_element_type=F32)
    return dot(lhs, high) + dot(lhs, low)


def tables_kernel(win_hbm, mix_hbm, win_ref, mix_ref, sems):
    member = lax.axis_index("x") * 2 + lax.axis_index("core")
    p = lax.axis_index("zh") * N_XC + member
    copies = [
        pltpu.make_async_copy(win_hbm.at[member], win_ref, sems.at[0]),
        pltpu.make_async_copy(mix_hbm.at[p], mix_ref, sems.at[1]),
    ]
    for copy in copies:
        copy.start()
    for copy in copies:
        copy.wait()


def tables():
    return pl.pallas_call(
        tables_kernel,
        in_specs=[HBM, HBM],
        out_specs=[VMEM, VMEM],
        out_shape=[
            jax.ShapeDtypeStruct((BLK, 2 * LANE), BF),
            jax.ShapeDtypeStruct((4 * LANE, N_Q * N_XC * GROUP), BF),
        ],
        scratch_shapes=[pltpu.SemaphoreType.DMA((2,))],
        compiler_params=LITTLE,
        name="tables",
    )(in_hbm(jnp.asarray(window_table(), BF)), in_hbm(jnp.asarray(mix_table(), BF)))


def rotate_kernel(*refs):
    slots, (win_ref, mix_ref, out_ref) = refs[:RING], refs[RING:]
    member = lax.axis_index("x") * 2 + lax.axis_index("core")
    g = jnp.concatenate(
        [unpack(part) for ref in slots for part in (ref[: 2 * GROUP, :], ref[2 * GROUP :, :])],
        axis=0,
    ).astype(BF)
    window = win_ref[...]
    parts = []
    for j in range(N_Q):
        parts.append(
            jnp.dot(g[:, j * BLK : (j + 1) * BLK], window, preferred_element_type=F32)
        )
    spread = jnp.concatenate(parts, axis=0)
    lanes = lax.broadcasted_iota(jnp.int32, (LANE, LANE), 1)
    halves = []
    for z in range(2):
        start = ROWS * (member + N_XC * z)
        both = split_dot(
            mix_ref[z * 2 * LANE : (z + 1) * 2 * LANE, :], spread[:, z * LANE : (z + 1) * LANE]
        )
        wrapped = start % BLK + lanes >= BLK
        mixed = jnp.where(wrapped, both[LANE:], both[:LANE])
        halves.append(mixed.reshape(N_TOK, 1, GROUP, LANE))
    out_ref[...] = jnp.concatenate(halves, axis=1).reshape(2 * LANE, LANE)


def rotate(slots, window, mix):
    return pl.pallas_call(
        rotate_kernel,
        in_specs=[VMEM] * (RING + 2),
        out_specs=VMEM,
        out_shape=jax.ShapeDtypeStruct((2 * LANE, LANE), F32),
        compiler_params=LITTLE,
        name="rotate",
    )(*slots, window, mix)


def finish_kernel(x_ref, h_ref, out_ref):
    terms = x_ref[...].reshape(N_TOK, 2, GROUP, LANE)
    total = (terms[:, 0] + terms[:, 1]).reshape(COLS, LANE) * (1.0 / (FF * TOKENS))
    dims = (((0,), (0,)), ((), ()))
    dot = functools.partial(lax.dot_general, dimension_numbers=dims, preferred_element_type=F32)
    high = total.astype(BF)
    rest = total - high.astype(F32)
    mid = rest.astype(BF)
    low = (rest - mid.astype(F32)).astype(BF)
    table = h_ref[...]
    result = dot(high, table) + (dot(mid, table) + dot(low, table))
    out_ref[...] = result[:ROWS]


def finish(x, table):
    return pl.pallas_call(
        finish_kernel,
        in_specs=[VMEM, VMEM],
        out_specs=VMEM,
        out_shape=jax.ShapeDtypeStruct((ROWS, COLS), F32),
        compiler_params=LITTLE,
        name="finish",
    )(x, table)


def shift(x, axis, s):
    return lax.ppermute(x, axis, [(i, (i + s) % RING) for i in range(RING)])


def swap(x, axis):
    return lax.ppermute(x, axis, [(0, 1), (1, 0)])


def body(hidden, signs):
    send, keep, held, sign = fold(hidden, signs.reshape(N_L, LANE))
    pair, short = sum_core(keep, swap(send, "core"))
    mine = sum_x(pair, [shift(short, "x", s) for s in (1, 3, 2)])
    mine_z = swap(mine, "zh")
    acc = outer(mine, swap(mine, "core"), held)
    acc = outer_mine(mine_z, acc, held)
    own, *sends = outer_other(swap(mine_z, "core"), acc, held)

    own, *sends = sum_y(own, [shift(sends[s - 1], "y", s) for s in (1, 3, 2)])
    g = sum_z(own, [shift(x, "zl", s + 1) for s, x in enumerate(sends)], sign)

    g = pair_up(g, swap(g, "core"))
    turned = rotate([g] + [shift(g, "x", s) for s in (1, 2, 3)], *tables())
    turned = lax.all_to_all(turned, ("y", "zl", "zh"), split_axis=0, concat_axis=0, tiled=True)
    return finish(turned, jnp.asarray(sylvester(COLS), BF))


def solution(mesh):
    fine = Mesh(mesh.devices.reshape(4, 4, 2, 4, 2), ("y", "zl", "zh", "x", "core"))
    return jax.shard_map(
        body,
        mesh=fine,
        in_specs=(P(TOK_AXES, TP_AXES), P(TP_AXES)),
        out_specs=P(TOK_AXES + TP_AXES, None),
        check_vma=False,
    )
```
